32 devices in a mesh: groups: 2 (over x), seq: 16 (over z, y, core).
Axes of the slice: x: 2, y: 2, z: 4, core: 2. Of those that a mesh axis runs over, the one named last changes fastest.
Arguments:
- query: bfloat16 [4096, 4096], P(('groups', 'seq')), parts along dimension 0, may hold values from -6 to 6
- key_in: bfloat16 [4096, 4096], P(('groups', 'seq')), parts along dimension 0, may hold values from -6 to 6
- value: bfloat16 [4096, 4096], P(('groups', 'seq')), parts along dimension 0, may hold values from -6 to 6
- q_gain: float32 [4096], replicated, may hold values from 0.25 to 1.75
- k_gain: float32 [4096], replicated, may hold values from 0.25 to 1.75
- tile_list: int32 [32, 16, 3], replicated, may hold values from 0 to 15, as said below
- tile_count: int32 [32, 16], replicated, may hold values from 1 to 3, as said below
Outputs:
- attended: bfloat16 [4096, 4096], P(('groups', 'seq')), parts along dimension 0
The draws below stay inside these ranges and needn't reach their ends.
There are 2 independent parts, one for each index of `groups`. The reference program is written for one: setup_inputs(seed, part) draws one part's arguments, and reference() takes and returns one part's arrays. A program takes and returns all parts, laid end to end along the dimension named above; an argument that names none is the same for every part. Nothing has to cross between parts.
Inputs may be any that keep to these rules, and one draw needn't show every extreme that they name: `tile_list`: the first entry of every list is the query block itself; the used entries of a list are distinct; unused entries also hold block numbers. `tile_count`: some list uses all 3 entries in every draw.
All inputs are finite; a program needn't handle non-finite values.
Results may differ from the reference program's by a relative error of at most 0.0086.
Values may be sent and summed in bfloat16 or wider, within the bound.
A program may use at most 128 MiB of HBM per device.

```python
import jax
import jax.numpy as jnp
from jax import lax

HEADS = 32
HEAD_DIM = 128
BLOCK = 128
WIDTH = 4096
SEQ = 2048
KMAX = 3


def rough_field(key):
    key_val = jax.random.fold_in(key, 0)
    values = jax.random.normal(key_val, (SEQ, HEADS * HEAD_DIM), jnp.float32)
    return jnp.clip(values, -6.0, 6.0)


def draw_query(key, part):
    key = jax.random.fold_in(key, 11)
    key_field = jax.random.fold_in(key, 0)
    values = rough_field(key_field)
    return values.astype(jnp.bfloat16)


def draw_key_in(key, part):
    key = jax.random.fold_in(key, 12)
    key_field = jax.random.fold_in(key, 0)
    values = rough_field(key_field)
    return values.astype(jnp.bfloat16)


def tile_tables(key):
    key_caps, key_rows, key_order, key_heavy, key_spot = jax.random.split(key, 5)
    blocks = SEQ // BLOCK
    head_caps = jax.random.randint(key_caps, (HEADS,), (KMAX + 1) // 2, KMAX + 1)
    heavy_head = jax.random.randint(key_heavy, (), 0, HEADS)
    head_caps = jnp.where(jnp.arange(HEADS) == heavy_head, KMAX, head_caps)
    lowest = jnp.maximum(1, head_caps // 2)
    counts = jax.random.randint(key_rows, (HEADS, blocks), lowest[:, None], head_caps[:, None] + 1)
    peak_block = jax.random.randint(key_spot, (), 0, blocks)
    counts = counts.at[heavy_head, peak_block].set(KMAX)
    order_noise = jax.random.randint(key_order, (HEADS, blocks, blocks), 0, 2 ** 15) * blocks + jnp.arange(blocks)[None, None, :]
    diagonal = jnp.arange(blocks)[:, None] == jnp.arange(blocks)[None, :]
    ranking = jnp.where(diagonal[None], 2 ** 30, order_noise)
    tile_slots = lax.top_k(ranking, KMAX)[1].astype(jnp.int32)
    return (tile_slots, counts.astype(jnp.int32))


def draw_tile_list(key, part):
    tile_slots, counts = tile_tables(key)
    return tile_slots


def draw_tile_count(key, part):
    tile_slots, counts = tile_tables(key)
    return counts


def block_levels(stream_key, shape, pieces, least, top_value):
    gain = 1.0
    for dim, blocks in pieces:
        draws = jax.random.uniform(jax.random.fold_in(jax.random.fold_in(stream_key, 6), dim), (blocks,), jnp.float32, least / len(pieces), top_value / len(pieces))
        gain = gain * jnp.repeat(jnp.exp(draws), shape[dim] // blocks).reshape((-1,) + (1,) * (len(shape) - 1 - dim))
    return gain


def normal_values(stream_key, dims, scale, limit, cuts=(), held_as=jnp.bfloat16):
    drawn = scale * jax.random.normal(stream_key, dims, jnp.float32)
    if cuts:
        drawn = drawn * block_levels(stream_key, dims, cuts, -0.22, 0.18)
    return jnp.clip(drawn, -limit, limit).astype(held_as)


def setup_inputs(seed: int = 0, part: int = 0) -> dict:
    key_of = jax.random.split(jax.random.key(seed), 8)
    own_keys = jax.random.split(jax.random.fold_in(key_of[7], part), 8)
    return {
        "query": draw_query(jax.random.fold_in(jax.random.fold_in(key_of[7], part), 71), part),
        "key_in": draw_key_in(jax.random.fold_in(jax.random.fold_in(key_of[7], part), 71), part),
        "value": normal_values(own_keys[2], (SEQ, WIDTH), 1.0, 6.0, ((0, 16),)),
        "q_gain": jnp.clip(1.0 + 0.15 * jax.random.normal(key_of[3], (WIDTH,), jnp.float32), 0.25, 1.75),
        "k_gain": jnp.clip(1.0 + 0.15 * jax.random.normal(key_of[4], (WIDTH,), jnp.float32), 0.25, 1.75),
        "tile_list": draw_tile_list(jax.random.fold_in(key_of[7], 71), part),
        "tile_count": draw_tile_count(jax.random.fold_in(key_of[7], 71), part),
    }


EPSILON = 1e-06

def rms_scaled(row_data, gain_row):
    values = row_data.astype(jnp.float32)
    power = lax.optimization_barrier(jnp.mean(values * values, axis=-1, keepdims=True))
    return (values * lax.rsqrt(power + EPSILON) * gain_row).astype(jnp.bfloat16)

def reference(query, key_in, value, q_gain, k_gain, tile_list, tile_count):
    q_normed = rms_scaled(query, q_gain)
    k_normed = rms_scaled(key_in, k_gain)
    blocks = SEQ // BLOCK
    logit_scale = HEAD_DIM ** (-0.5)

    def split_heads(row_data):
        return row_data.reshape(blocks, BLOCK, HEADS, HEAD_DIM).transpose(2, 0, 1, 3)

    def one_head(inputs):
        query_head, k_head, v_head, tile_slots, filled = inputs
        gathered_key_tiles = k_head[tile_slots].reshape(blocks, KMAX * BLOCK, HEAD_DIM).astype(jnp.float32)
        gathered_value_tiles = v_head[tile_slots].reshape(blocks, KMAX * BLOCK, HEAD_DIM).astype(jnp.float32)
        tile_scores = jnp.einsum('zia,zla->zil', query_head.astype(jnp.float32), gathered_key_tiles) * logit_scale
        is_valid = jnp.repeat(jnp.arange(KMAX)[None, :] < filled[:, None], BLOCK, axis=1)[:, None, :]
        row_max = lax.optimization_barrier(jnp.max(jnp.where(is_valid, tile_scores, -jnp.inf), axis=-1, keepdims=True))
        weights_f = jnp.where(is_valid, jnp.exp(tile_scores - row_max), 0.0)
        row_total = lax.optimization_barrier(jnp.sum(weights_f, axis=-1, keepdims=True))
        rounded_scores = lax.optimization_barrier(weights_f.astype(jnp.bfloat16)).astype(jnp.float32)
        weighted_values = jnp.einsum('ngi,nil->ngl', rounded_scores, gathered_value_tiles)
        return (weighted_values / row_total).astype(jnp.bfloat16)
    outputs = lax.map(one_head, (split_heads(q_normed), split_heads(k_normed), split_heads(value), tile_list, tile_count))
    return outputs.transpose(1, 2, 0, 3).reshape(SEQ, HEADS * HEAD_DIM)
```

```python
import functools
import math

import jax
import jax.numpy as jnp
from jax import lax
from jax.experimental import pallas as pl
from jax.experimental.pallas import tpu as pltpu
from jax.sharding import PartitionSpec as P

HEAD_DIM = 128
BLOCK = 128
ROW_TILE = 16
EPSILON = 1e-06
MESH = pl.DeviceIdType.MESH


def attention_kernel(
    n,
    heads_dev,
    slot_count,
    list_hbm,
    count_hbm,
    q_gain,
    k_gain,
    q_hbm,
    k_hbm,
    v_hbm,
    out,
    list_smem,
    count_smem,
    q_in,
    k_in,
    q_send,
    k_send,
    q_all,
    k_all,
    v_all,
    o_send,
    load_sem,
    own_sem,
    send_sem,
    recv_sem,
    back_send_sem,
    back_recv_sem,
):
    me = lax.axis_index("seq")
    heads = n * heads_dev
    width = heads * HEAD_DIM
    logit_scale = HEAD_DIM ** (-0.5)
    my_heads = pl.ds(me * heads_dev, heads_dev)

    loads = [
        pltpu.make_async_copy(q_hbm, q_in, load_sem.at[0]),
        pltpu.make_async_copy(k_hbm, k_in, load_sem.at[1]),
        pltpu.make_async_copy(list_hbm.at[my_heads], list_smem, load_sem.at[2]),
        pltpu.make_async_copy(count_hbm.at[my_heads], count_smem, load_sem.at[3]),
    ]
    for load in loads:
        load.start()

    barrier = pltpu.get_barrier_semaphore()

    def greet(i, carry):
        peer = lax.rem(me + 1 + i, n)
        pl.semaphore_signal(barrier, inc=1, device_id={"seq": peer}, device_id_type=MESH)
        return carry

    lax.fori_loop(0, n - 1, greet, 0)
    pl.semaphore_wait(barrier, n - 1)

    def partner(i):
        return lax.rem(me + 1 + lax.rem(n // 2 - 1 + i, n - 1), n)

    def v_columns(head):
        return v_hbm.at[:, pl.ds(pl.multiple_of(head * HEAD_DIM, HEAD_DIM), HEAD_DIM)]

    def out_columns(head):
        return out.at[:, pl.ds(pl.multiple_of(head * HEAD_DIM, HEAD_DIM), HEAD_DIM)]

    sources = (
        (v_columns, v_all),
        (lambda head: q_send.at[head], q_all),
        (lambda head: k_send.at[head], k_all),
    )

    def own_copy(kind, h):
        source, landing = sources[kind]
        return pltpu.make_async_copy(
            source(me * heads_dev + h), landing[h].at[me], own_sem.at[kind, h]
        )

    def spread(kind, h):
        source, landing = sources[kind]

        def body(i, carry):
            peer = partner(i)
            pltpu.make_async_remote_copy(
                src_ref=source(peer * heads_dev + h),
                dst_ref=landing[h].at[me],
                send_sem=send_sem.at[kind, h],
                recv_sem=recv_sem.at[kind, h],
                device_id={"seq": peer},
                device_id_type=MESH,
            ).start()
            return carry

        lax.fori_loop(0, n - 1, body, 0)
        own_copy(kind, h).start()

    def normalise(source, gain, target):
        def rows_step(i, carry):
            rows = pl.ds(pl.multiple_of(i * ROW_TILE, ROW_TILE), ROW_TILE)
            squares = jnp.zeros((ROW_TILE, HEAD_DIM), jnp.float32)
            for head in range(heads):
                part = source[rows, head * HEAD_DIM : (head + 1) * HEAD_DIM].astype(jnp.float32)
                squares = squares + part * part
            power = jnp.sum(squares, axis=-1, keepdims=True) / width
            scale = lax.rsqrt(power + EPSILON)
            for head in range(heads):
                columns = slice(head * HEAD_DIM, (head + 1) * HEAD_DIM)
                part = source[rows, columns].astype(jnp.float32)
                target[head, rows, :] = (part * scale * gain[:, columns]).astype(jnp.bfloat16)
            return carry

        lax.fori_loop(0, BLOCK // ROW_TILE, rows_step, 0)

    spread(0, 0)
    loads[0].wait()
    normalise(q_in, q_gain, q_send)
    spread(1, 0)
    loads[1].wait()
    normalise(k_in, k_gain, k_send)
    spread(2, 0)
    for h in range(1, heads_dev):
        for kind in range(3):
            spread(kind, h)
    loads[2].wait()
    loads[3].wait()

    def landed(buffer, semaphore):
        others = buffer.at[pl.ds(0, n - 1)]
        pltpu.make_async_copy(others, others, semaphore).wait()

    def attend(h, block):
        filled = count_smem[h, block]
        queries = q_all[h][block]
        scores = []
        for slot in range(slot_count):
            tile = list_smem[h, block, slot]
            tile_scores = (
                lax.dot_general(
                    queries,
                    k_all[h][tile],
                    (((1,), (1,)), ((), ())),
                    preferred_element_type=jnp.float32,
                )
                * logit_scale
            )
            if slot > 0:
                tile_scores = jnp.where(
                    jnp.full(tile_scores.shape, filled, jnp.int32) > slot, tile_scores, -jnp.inf
                )
            scores.append(tile_scores)
        row_max = jnp.max(functools.reduce(jnp.maximum, scores), axis=-1, keepdims=True)
        weights = [jnp.exp(tile_scores - row_max) for tile_scores in scores]
        row_total = jnp.sum(functools.reduce(jnp.add, weights), axis=-1, keepdims=True)
        total = None
        for slot in range(slot_count):
            tile = list_smem[h, block, slot]
            product = jnp.dot(
                weights[slot].astype(jnp.bfloat16),
                v_all[h][tile],
                preferred_element_type=jnp.float32,
            )
            total = product if total is None else total + product
        return (total / row_total).astype(jnp.bfloat16)

    for h in range(heads_dev):
        for kind in range(3):
            own_copy(kind, h).wait()
            landed(sources[kind][1][h], recv_sem.at[kind, h])

        def item(i, carry):
            block = partner(i)
            o_send[h, block] = attend(h, block)
            pltpu.make_async_remote_copy(
                src_ref=o_send.at[h, block],
                dst_ref=out_columns(me * heads_dev + h),
                send_sem=back_send_sem.at[h],
                recv_sem=back_recv_sem.at[h],
                device_id={"seq": block},
                device_id_type=MESH,
            ).start()
            return carry

        lax.fori_loop(0, n - 1, item, 0, unroll=UNROLL)
        o_send[h, me] = attend(h, me)
        pltpu.make_async_copy(
            o_send.at[h, me], out_columns(me * heads_dev + h), own_sem.at[3, h]
        ).start()

    for h in range(heads_dev):
        pltpu.make_async_copy(
            o_send.at[h, me], out_columns(me * heads_dev + h), own_sem.at[3, h]
        ).wait()
        landed(o_send.at[h], back_recv_sem.at[h])
        landed(o_send.at[h], back_send_sem.at[h])
        for kind in range(3):
            landed(sources[kind][1][h], send_sem.at[kind, h])


UNROLL = 3


def fused(query, key_in, value, q_gain, k_gain, tile_list, tile_count):
    n = lax.axis_size("seq")
    tok_rows, row_width = query.shape
    head_count = row_width // HEAD_DIM
    heads_dev = head_count // n
    slot_count = tile_list.shape[-1]
    blocks = tile_list.shape[1]
    any_space = pl.BlockSpec(memory_space=pl.ANY)
    in_vmem = pl.BlockSpec(memory_space=pltpu.VMEM)
    landing = (pltpu.VMEM((n, BLOCK, HEAD_DIM), jnp.bfloat16),) * heads_dev
    return pl.pallas_call(
        functools.partial(attention_kernel, n, heads_dev, slot_count),
        out_shape=jax.ShapeDtypeStruct((tok_rows, row_width), jnp.bfloat16),
        in_specs=[any_space, any_space, in_vmem, in_vmem, any_space, any_space, any_space],
        out_specs=any_space,
        scratch_shapes=[
            pltpu.SMEM((heads_dev, blocks, slot_count), jnp.int32),
            pltpu.SMEM((heads_dev, blocks), jnp.int32),
            pltpu.VMEM((tok_rows, row_width), jnp.bfloat16),
            pltpu.VMEM((tok_rows, row_width), jnp.bfloat16),
            pltpu.VMEM((head_count, BLOCK, HEAD_DIM), jnp.bfloat16),
            pltpu.VMEM((head_count, BLOCK, HEAD_DIM), jnp.bfloat16),
            landing,
            landing,
            landing,
            pltpu.VMEM((heads_dev, n, BLOCK, HEAD_DIM), jnp.bfloat16),
            pltpu.SemaphoreType.DMA((4,)),
            pltpu.SemaphoreType.DMA((4, heads_dev)),
            pltpu.SemaphoreType.DMA((3, heads_dev)),
            pltpu.SemaphoreType.DMA((3, heads_dev)),
            pltpu.SemaphoreType.DMA((heads_dev,)),
            pltpu.SemaphoreType.DMA((heads_dev,)),
        ],
        compiler_params=pltpu.CompilerParams(
            collective_id=0, has_side_effects=True, vmem_limit_bytes=48 * 1024 * 1024
        ),
        cost_estimate=pl.CostEstimate(
            flops=4 * heads_dev * n * slot_count * BLOCK * BLOCK * HEAD_DIM,
            bytes_accessed=8 * tok_rows * row_width,
            transcendentals=heads_dev * n * slot_count * BLOCK * BLOCK,
        ),
    )(
        tile_list,
        tile_count,
        q_gain.reshape(1, row_width),
        k_gain.reshape(1, row_width),
        query,
        key_in,
        value,
    )


def rms_scaled(row_data, gain_row):
    values = row_data.astype(jnp.float32)
    power = jnp.mean(values * values, axis=-1, keepdims=True)
    return (values * lax.rsqrt(power + EPSILON) * gain_row).astype(jnp.bfloat16)


def exchanged(query, key_in, value, q_gain, k_gain, tile_list, tile_count):
    devices = lax.axis_size("seq")
    tok_rows, row_width = query.shape
    head_dim = HEAD_DIM
    block_rows = BLOCK
    head_count = row_width // head_dim
    replicas = max(1, devices // head_count)
    heads_dev = max(1, head_count // devices)
    group_count = head_count // heads_dev
    slot_count = tile_list.shape[-1]
    blocks = tile_list.shape[1]
    position = lax.axis_index("seq")
    residue = position % replicas
    head_group = position // replicas
    logit_scale = head_dim ** (-0.5)
    q_normed = rms_scaled(query, q_gain)
    k_normed = rms_scaled(key_in, k_gain)

    def whole_rows(row_data):
        split = row_data.reshape(tok_rows, group_count, 1, heads_dev, head_dim)
        spread = jnp.broadcast_to(split, (tok_rows, group_count, replicas, heads_dev, head_dim))
        return spread.transpose(1, 2, 3, 0, 4).reshape(devices, heads_dev, tok_rows, head_dim)

    stacked = jnp.stack([whole_rows(q_normed), whole_rows(k_normed), whole_rows(value)], axis=1)
    received = lax.all_to_all(stacked, "seq", split_axis=0, concat_axis=0, tiled=True)
    full_rows = received.transpose(1, 2, 0, 3, 4).reshape(
        3, heads_dev, devices * tok_rows, head_dim
    )
    own_blocks = blocks // replicas
    query_sets = full_rows[0].reshape(heads_dev, own_blocks, replicas, block_rows, head_dim)
    queries = lax.dynamic_index_in_dim(query_sets, residue, axis=2, keepdims=False)
    queries = queries.reshape(heads_dev * own_blocks, block_rows, head_dim)
    query_block = jnp.arange(own_blocks) * replicas + residue
    head_ids = head_group * heads_dev + jnp.arange(heads_dev)
    item_slots = (
        tile_list[head_ids][:, query_block] + (jnp.arange(heads_dev) * blocks)[:, None, None]
    )
    item_slots = item_slots.reshape(-1, slot_count)
    counts = tile_count[head_ids][:, query_block].reshape(-1)
    key_tiles_all = full_rows[1].reshape(heads_dev * blocks, block_rows, head_dim)
    value_tiles_all = full_rows[2].reshape(heads_dev * blocks, block_rows, head_dim)
    item_count = queries.shape[0]
    per_step = math.gcd(item_count, max(1, 512 // block_rows))

    def padded(q_items, tile_slots, filled):
        gathered_key_tiles = jnp.take(key_tiles_all, tile_slots, axis=0).reshape(
            per_step, slot_count * block_rows, head_dim
        )
        gathered_value_tiles = jnp.take(value_tiles_all, tile_slots, axis=0).reshape(
            per_step, slot_count * block_rows, head_dim
        )
        tile_scores = (
            jnp.einsum(
                "gqd,gkd->gqk", q_items, gathered_key_tiles, preferred_element_type=jnp.float32
            )
            * logit_scale
        )
        is_valid = jnp.repeat(
            jnp.arange(slot_count)[None, :] < filled[:, None], block_rows, axis=1
        )[:, None, :]
        row_max = jnp.max(jnp.where(is_valid, tile_scores, -jnp.inf), axis=-1, keepdims=True)
        weights_f = jnp.where(is_valid, jnp.exp(tile_scores - row_max), 0.0)
        row_total = jnp.sum(weights_f, axis=-1, keepdims=True)
        weighted_values = jnp.einsum(
            "gqk,gkd->gqd",
            weights_f.astype(jnp.bfloat16),
            gathered_value_tiles,
            preferred_element_type=jnp.float32,
        )
        return (weighted_values / row_total).astype(jnp.bfloat16)

    def attend(batch_in):
        q_items, tile_slots, filled = batch_in
        return padded(q_items, tile_slots, filled)

    steps_n = item_count // per_step
    outputs = lax.map(
        attend,
        (
            queries.reshape(steps_n, per_step, block_rows, head_dim),
            item_slots.reshape(steps_n, per_step, slot_count),
            counts.reshape(steps_n, per_step),
        ),
    )
    outputs = outputs.reshape(heads_dev, own_blocks, 1, block_rows, head_dim)
    chosen = (jnp.arange(replicas) == residue).astype(jnp.bfloat16)[None, None, :, None, None]
    placed = (
        (outputs * chosen).reshape(heads_dev, devices, tok_rows, head_dim).transpose(1, 0, 2, 3)
    )
    returned = lax.all_to_all(placed, "seq", split_axis=0, concat_axis=0, tiled=True)
    returned = returned.reshape(group_count, replicas, heads_dev, tok_rows, head_dim)
    combined = jnp.sum(returned.astype(jnp.float32), axis=1).astype(jnp.bfloat16)
    return combined.transpose(2, 0, 1, 3).reshape(tok_rows, row_width)


def per_device(query, key_in, value, q_gain, k_gain, tile_list, tile_count):
    devices = lax.axis_size("seq")
    tok_rows, row_width = query.shape
    head_count = row_width // HEAD_DIM
    one_block = tok_rows == BLOCK and tile_list.shape[1] == devices
    if devices > 1 and head_count % devices == 0 and one_block:
        return fused(query, key_in, value, q_gain, k_gain, tile_list, tile_count)
    return exchanged(query, key_in, value, q_gain, k_gain, tile_list, tile_count)


def solution(mesh):
    return jax.shard_map(
        per_device,
        mesh=mesh,
        in_specs=(
            P(("groups", "seq"), None),
            P(("groups", "seq"), None),
            P(("groups", "seq"), None),
            P(),
            P(),
            P(),
            P(),
        ),
        out_specs=P(("groups", "seq"), None),
        check_vma=False,
    )
```

```python
import functools
import math

import jax
import jax.numpy as jnp
from jax import lax
from jax.experimental import pallas as pl
from jax.experimental.pallas import tpu as pltpu
from jax.sharding import PartitionSpec as P

HEAD_DIM = 128
BLOCK = 128
ROW_TILE = 16
EPSILON = 1e-06
MESH = pl.DeviceIdType.MESH


def attention_kernel(
    n,
    heads_dev,
    slot_count,
    list_hbm,
    count_hbm,
    q_gain_hbm,
    k_gain_hbm,
    q_hbm,
    k_hbm,
    v_hbm,
    out,
    list_smem,
    count_smem,
    q_gain,
    k_gain,
    q_in,
    k_in,
    q_send,
    k_send,
    q_all,
    k_all,
    v_all,
    o_send,
    load_sem,
    own_sem,
    send_sem,
    recv_sem,
    back_send_sem,
    back_recv_sem,
):
    me = lax.axis_index("seq")
    heads = n * heads_dev
    width = heads * HEAD_DIM
    logit_scale = HEAD_DIM ** (-0.5)

    loads = [
        pltpu.make_async_copy(q_hbm, q_in, load_sem.at[0]),
        pltpu.make_async_copy(q_gain_hbm, q_gain, load_sem.at[1]),
        pltpu.make_async_copy(k_hbm, k_in, load_sem.at[2]),
        pltpu.make_async_copy(k_gain_hbm, k_gain, load_sem.at[3]),
        pltpu.make_async_copy(list_hbm, list_smem, load_sem.at[4]),
        pltpu.make_async_copy(count_hbm, count_smem, load_sem.at[5]),
    ]
    for load in loads:
        load.start()

    barrier = pltpu.get_barrier_semaphore()

    def greet(i, carry):
        peer = lax.rem(me + 1 + i, n)
        pl.semaphore_signal(barrier, inc=1, device_id={"seq": peer}, device_id_type=MESH)
        return carry

    lax.fori_loop(0, n - 1, greet, 0)
    pl.semaphore_wait(barrier, n - 1)

    def partner(i):
        return lax.rem(me + 1 + lax.rem(n // 2 - 1 + i, n - 1), n)

    def v_columns(head):
        return v_hbm.at[:, pl.ds(pl.multiple_of(head * HEAD_DIM, HEAD_DIM), HEAD_DIM)]

    def out_columns(head):
        return out.at[:, pl.ds(pl.multiple_of(head * HEAD_DIM, HEAD_DIM), HEAD_DIM)]

    sources = (
        (v_columns, v_all),
        (lambda head: q_send.at[head], q_all),
        (lambda head: k_send.at[head], k_all),
    )

    def own_copy(kind, h):
        source, landing = sources[kind]
        return pltpu.make_async_copy(
            source(me * heads_dev + h), landing[h].at[me], own_sem.at[kind, h]
        )

    def spread(kind, h):
        source, landing = sources[kind]

        def body(i, carry):
            peer = partner(i)
            pltpu.make_async_remote_copy(
                src_ref=source(peer * heads_dev + h),
                dst_ref=landing[h].at[me],
                send_sem=send_sem.at[kind, h],
                recv_sem=recv_sem.at[kind, h],
                device_id={"seq": peer},
                device_id_type=MESH,
            ).start()
            return carry

        lax.fori_loop(0, n - 1, body, 0)
        own_copy(kind, h).start()

    def normalise(source, gain, target):
        def rows_step(i, carry):
            rows = pl.ds(pl.multiple_of(i * ROW_TILE, ROW_TILE), ROW_TILE)
            squares = jnp.zeros((ROW_TILE, HEAD_DIM), jnp.float32)
            for head in range(heads):
                part = source[rows, head * HEAD_DIM : (head + 1) * HEAD_DIM].astype(jnp.float32)
                squares = squares + part * part
            power = jnp.sum(squares, axis=-1, keepdims=True) / width
            scale = lax.rsqrt(power + EPSILON)
            for head in range(heads):
                columns = slice(head * HEAD_DIM, (head + 1) * HEAD_DIM)
                part = source[rows, columns].astype(jnp.float32)
                target[head, rows, :] = (part * scale * gain[:, columns]).astype(jnp.bfloat16)
            return carry

        lax.fori_loop(0, BLOCK // ROW_TILE, rows_step, 0)

    spread(0, 0)
    loads[0].wait()
    loads[1].wait()
    normalise(q_in, q_gain, q_send)
    spread(1, 0)
    loads[2].wait()
    loads[3].wait()
    normalise(k_in, k_gain, k_send)
    spread(2, 0)
    for h in range(1, heads_dev):
        for kind in range(3):
            spread(kind, h)
    loads[4].wait()
    loads[5].wait()

    def landed(buffer, semaphore):
        others = buffer.at[pl.ds(0, n - 1)]
        pltpu.make_async_copy(others, others, semaphore).wait()

    def attend(h, block):
        filled = count_smem[block, me * heads_dev + h]
        queries = q_all[h][block]
        scores = []
        for slot in range(slot_count):
            tile = list_smem[slot, block, me * heads_dev + h]
            tile_scores = (
                lax.dot_general(
                    queries,
                    k_all[h][tile],
                    (((1,), (1,)), ((), ())),
                    preferred_element_type=jnp.float32,
                )
                * logit_scale
            )
            if slot > 0:
                tile_scores = jnp.where(
                    jnp.full(tile_scores.shape, filled, jnp.int32) > slot, tile_scores, -jnp.inf
                )
            scores.append(tile_scores)
        row_max = jnp.max(functools.reduce(jnp.maximum, scores), axis=-1, keepdims=True)
        weights = [jnp.exp(tile_scores - row_max) for tile_scores in scores]
        row_total = jnp.sum(functools.reduce(jnp.add, weights), axis=-1, keepdims=True)
        total = None
        for slot in range(slot_count):
            tile = list_smem[slot, block, me * heads_dev + h]
            product = jnp.dot(
                weights[slot].astype(jnp.bfloat16),
                v_all[h][tile],
                preferred_element_type=jnp.float32,
            )
            total = product if total is None else total + product
        return (total / row_total).astype(jnp.bfloat16)

    def returned(h, block):
        return pltpu.make_async_remote_copy(
            src_ref=o_send.at[h, block],
            dst_ref=out_columns(me * heads_dev + h),
            send_sem=back_send_sem.at[h],
            recv_sem=back_recv_sem.at[h],
            device_id={"seq": block},
            device_id_type=MESH,
        )

    def kept(h):
        return pltpu.make_async_copy(
            o_send.at[h, me], out_columns(me * heads_dev + h), own_sem.at[3, h]
        )

    last = heads_dev - 1
    for h in range(heads_dev):
        for kind in range(3):
            own_copy(kind, h).wait()
            landed(sources[kind][1][h], recv_sem.at[kind, h])

        def item(i, carry):
            block = partner(i)
            o_send[h, block] = attend(h, block)
            if h == last:
                returned(h, block).start()
            return carry

        lax.fori_loop(0, n - 1, item, 0, unroll=UNROLL)
        o_send[h, me] = attend(h, me)
        kept(h).start()
        if h == last - 1:
            for kind in range(3):
                landed(sources[kind][1][last], send_sem.at[kind, last])

            def give_back(i, carry):
                for done in range(last):
                    returned(done, partner(i)).start()
                return carry

            lax.fori_loop(0, n - 1, give_back, 0)

    for h in range(heads_dev):
        kept(h).wait()
        landed(o_send.at[h], back_recv_sem.at[h])
        landed(o_send.at[h], back_send_sem.at[h])
        if h < last or last == 0:
            for kind in range(3):
                landed(sources[kind][1][h], send_sem.at[kind, h])


UNROLL = 3


def fused(query, key_in, value, q_gain, k_gain, tile_list, tile_count):
    n = lax.axis_size("seq")
    tok_rows, row_width = query.shape
    head_count = row_width // HEAD_DIM
    heads_dev = head_count // n
    slot_count = tile_list.shape[-1]
    blocks = tile_list.shape[1]
    any_space = pl.BlockSpec(memory_space=pl.ANY)
    landing = (pltpu.VMEM((n, BLOCK, HEAD_DIM), jnp.bfloat16),) * heads_dev
    return pl.pallas_call(
        functools.partial(attention_kernel, n, heads_dev, slot_count),
        out_shape=jax.ShapeDtypeStruct((tok_rows, row_width), jnp.bfloat16),
        in_specs=[any_space] * 7,
        out_specs=any_space,
        scratch_shapes=[
            pltpu.SMEM((slot_count, blocks, head_count), jnp.int32),
            pltpu.SMEM((blocks, head_count), jnp.int32),
            pltpu.VMEM((1, row_width), jnp.float32),
            pltpu.VMEM((1, row_width), jnp.float32),
            pltpu.VMEM((tok_rows, row_width), jnp.bfloat16),
            pltpu.VMEM((tok_rows, row_width), jnp.bfloat16),
            pltpu.VMEM((head_count, BLOCK, HEAD_DIM), jnp.bfloat16),
            pltpu.VMEM((head_count, BLOCK, HEAD_DIM), jnp.bfloat16),
            landing,
            landing,
            landing,
            pltpu.VMEM((heads_dev, n, BLOCK, HEAD_DIM), jnp.bfloat16),
            pltpu.SemaphoreType.DMA((6,)),
            pltpu.SemaphoreType.DMA((4, heads_dev)),
            pltpu.SemaphoreType.DMA((3, heads_dev)),
            pltpu.SemaphoreType.DMA((3, heads_dev)),
            pltpu.SemaphoreType.DMA((heads_dev,)),
            pltpu.SemaphoreType.DMA((heads_dev,)),
        ],
        compiler_params=pltpu.CompilerParams(
            collective_id=0, has_side_effects=True, vmem_limit_bytes=60 * 1024 * 1024
        ),
        cost_estimate=pl.CostEstimate(
            flops=4 * heads_dev * n * slot_count * BLOCK * BLOCK * HEAD_DIM,
            bytes_accessed=8 * tok_rows * row_width,
            transcendentals=heads_dev * n * slot_count * BLOCK * BLOCK,
        ),
    )(
        tile_list.transpose(2, 1, 0),
        tile_count.T,
        q_gain.reshape(1, row_width),
        k_gain.reshape(1, row_width),
        query,
        key_in,
        value,
    )


def rms_scaled(row_data, gain_row):
    values = row_data.astype(jnp.float32)
    power = jnp.mean(values * values, axis=-1, keepdims=True)
    return (values * lax.rsqrt(power + EPSILON) * gain_row).astype(jnp.bfloat16)


def exchanged(query, key_in, value, q_gain, k_gain, tile_list, tile_count):
    devices = lax.axis_size("seq")
    tok_rows, row_width = query.shape
    head_dim = HEAD_DIM
    block_rows = BLOCK
    head_count = row_width // head_dim
    replicas = max(1, devices // head_count)
    heads_dev = max(1, head_count // devices)
    group_count = head_count // heads_dev
    slot_count = tile_list.shape[-1]
    blocks = tile_list.shape[1]
    position = lax.axis_index("seq")
    residue = position % replicas
    head_group = position // replicas
    logit_scale = head_dim ** (-0.5)
    q_normed = rms_scaled(query, q_gain)
    k_normed = rms_scaled(key_in, k_gain)

    def whole_rows(row_data):
        split = row_data.reshape(tok_rows, group_count, 1, heads_dev, head_dim)
        spread = jnp.broadcast_to(split, (tok_rows, group_count, replicas, heads_dev, head_dim))
        return spread.transpose(1, 2, 3, 0, 4).reshape(devices, heads_dev, tok_rows, head_dim)

    stacked = jnp.stack([whole_rows(q_normed), whole_rows(k_normed), whole_rows(value)], axis=1)
    received = lax.all_to_all(stacked, "seq", split_axis=0, concat_axis=0, tiled=True)
    full_rows = received.transpose(1, 2, 0, 3, 4).reshape(
        3, heads_dev, devices * tok_rows, head_dim
    )
    own_blocks = blocks // replicas
    query_sets = full_rows[0].reshape(heads_dev, own_blocks, replicas, block_rows, head_dim)
    queries = lax.dynamic_index_in_dim(query_sets, residue, axis=2, keepdims=False)
    queries = queries.reshape(heads_dev * own_blocks, block_rows, head_dim)
    query_block = jnp.arange(own_blocks) * replicas + residue
    head_ids = head_group * heads_dev + jnp.arange(heads_dev)
    item_slots = (
        tile_list[head_ids][:, query_block] + (jnp.arange(heads_dev) * blocks)[:, None, None]
    )
    item_slots = item_slots.reshape(-1, slot_count)
    counts = tile_count[head_ids][:, query_block].reshape(-1)
    key_tiles_all = full_rows[1].reshape(heads_dev * blocks, block_rows, head_dim)
    value_tiles_all = full_rows[2].reshape(heads_dev * blocks, block_rows, head_dim)
    item_count = queries.shape[0]
    per_step = math.gcd(item_count, max(1, 512 // block_rows))

    def padded(q_items, tile_slots, filled):
        gathered_key_tiles = jnp.take(key_tiles_all, tile_slots, axis=0).reshape(
            per_step, slot_count * block_rows, head_dim
        )
        gathered_value_tiles = jnp.take(value_tiles_all, tile_slots, axis=0).reshape(
            per_step, slot_count * block_rows, head_dim
        )
        tile_scores = (
            jnp.einsum(
                "gqd,gkd->gqk", q_items, gathered_key_tiles, preferred_element_type=jnp.float32
            )
            * logit_scale
        )
        is_valid = jnp.repeat(
            jnp.arange(slot_count)[None, :] < filled[:, None], block_rows, axis=1
        )[:, None, :]
        row_max = jnp.max(jnp.where(is_valid, tile_scores, -jnp.inf), axis=-1, keepdims=True)
        weights_f = jnp.where(is_valid, jnp.exp(tile_scores - row_max), 0.0)
        row_total = jnp.sum(weights_f, axis=-1, keepdims=True)
        weighted_values = jnp.einsum(
            "gqk,gkd->gqd",
            weights_f.astype(jnp.bfloat16),
            gathered_value_tiles,
            preferred_element_type=jnp.float32,
        )
        return (weighted_values / row_total).astype(jnp.bfloat16)

    def attend(batch_in):
        q_items, tile_slots, filled = batch_in
        return padded(q_items, tile_slots, filled)

    steps_n = item_count // per_step
    outputs = lax.map(
        attend,
        (
            queries.reshape(steps_n, per_step, block_rows, head_dim),
            item_slots.reshape(steps_n, per_step, slot_count),
            counts.reshape(steps_n, per_step),
        ),
    )
    outputs = outputs.reshape(heads_dev, own_blocks, 1, block_rows, head_dim)
    chosen = (jnp.arange(replicas) == residue).astype(jnp.bfloat16)[None, None, :, None, None]
    placed = (
        (outputs * chosen).reshape(heads_dev, devices, tok_rows, head_dim).transpose(1, 0, 2, 3)
    )
    returned = lax.all_to_all(placed, "seq", split_axis=0, concat_axis=0, tiled=True)
    returned = returned.reshape(group_count, replicas, heads_dev, tok_rows, head_dim)
    combined = jnp.sum(returned.astype(jnp.float32), axis=1).astype(jnp.bfloat16)
    return combined.transpose(2, 0, 1, 3).reshape(tok_rows, row_width)


def per_device(query, key_in, value, q_gain, k_gain, tile_list, tile_count):
    devices = lax.axis_size("seq")
    tok_rows, row_width = query.shape
    head_count = row_width // HEAD_DIM
    one_block = tok_rows == BLOCK and tile_list.shape[1] == devices
    if devices > 1 and head_count % devices == 0 and one_block:
        return fused(query, key_in, value, q_gain, k_gain, tile_list, tile_count)
    return exchanged(query, key_in, value, q_gain, k_gain, tile_list, tile_count)


def solution(mesh):
    return jax.shard_map(
        per_device,
        mesh=mesh,
        in_specs=(
            P(("groups", "seq"), None),
            P(("groups", "seq"), None),
            P(("groups", "seq"), None),
            P(),
            P(),
            P(),
            P(),
        ),
        out_specs=P(("groups", "seq"), None),
        check_vma=False,
    )
```

```python
import functools
import math

import jax
import jax.numpy as jnp
from jax import lax
from jax.experimental import pallas as pl
from jax.experimental.pallas import tpu as pltpu
from jax.sharding import PartitionSpec as P

HEAD_DIM = 128
BLOCK = 128
ROW_TILE = 16
EPSILON = 1e-06
MESH = pl.DeviceIdType.MESH


def attention_kernel(
    n,
    heads_dev,
    slot_count,
    list_hbm,
    count_hbm,
    q_gain_hbm,
    k_gain_hbm,
    q_hbm,
    k_hbm,
    v_hbm,
    out,
    list_smem,
    count_smem,
    q_gain,
    k_gain,
    q_in,
    k_in,
    q_send,
    k_send,
    q_all,
    k_all,
    v_all,
    o_send,
    load_sem,
    own_sem,
    send_sem,
    recv_sem,
    back_send_sem,
    back_recv_sem,
):
    me = lax.axis_index("seq")
    heads = n * heads_dev
    width = heads * HEAD_DIM
    logit_scale = HEAD_DIM ** (-0.5)

    loads = [
        pltpu.make_async_copy(q_hbm, q_in, load_sem.at[0]),
        pltpu.make_async_copy(q_gain_hbm, q_gain, load_sem.at[1]),
        pltpu.make_async_copy(k_hbm, k_in, load_sem.at[2]),
        pltpu.make_async_copy(k_gain_hbm, k_gain, load_sem.at[3]),
        pltpu.make_async_copy(list_hbm, list_smem, load_sem.at[4]),
        pltpu.make_async_copy(count_hbm, count_smem, load_sem.at[5]),
    ]
    for load in loads:
        load.start()

    barrier = pltpu.get_barrier_semaphore()

    def greet(i, carry):
        peer = lax.rem(me + 1 + i, n)
        pl.semaphore_signal(barrier, inc=1, device_id={"seq": peer}, device_id_type=MESH)
        return carry

    lax.fori_loop(0, n - 1, greet, 0)
    pl.semaphore_wait(barrier, n - 1)

    def partner(i):
        return lax.rem(me + 1 + lax.rem(n // 2 - 1 + i, n - 1), n)

    def v_columns(head):
        return v_hbm.at[:, pl.ds(pl.multiple_of(head * HEAD_DIM, HEAD_DIM), HEAD_DIM)]

    def out_columns(head):
        return out.at[:, pl.ds(pl.multiple_of(head * HEAD_DIM, HEAD_DIM), HEAD_DIM)]

    sources = (
        (v_columns, v_all),
        (lambda head: q_send.at[head], q_all),
        (lambda head: k_send.at[head], k_all),
    )

    def own_copy(kind, h):
        source, landing = sources[kind]
        return pltpu.make_async_copy(
            source(me * heads_dev + h), landing[h].at[me], own_sem.at[kind, h]
        )

    def spread(kind, h):
        source, landing = sources[kind]

        def body(i, carry):
            peer = partner(i)
            pltpu.make_async_remote_copy(
                src_ref=source(peer * heads_dev + h),
                dst_ref=landing[h].at[me],
                send_sem=send_sem.at[kind, h],
                recv_sem=recv_sem.at[kind, h],
                device_id={"seq": peer},
                device_id_type=MESH,
            ).start()
            return carry

        lax.fori_loop(0, n - 1, body, 0)
        own_copy(kind, h).start()

    def normalise(source, gain, target):
        def rows_step(i, carry):
            rows = pl.ds(pl.multiple_of(i * ROW_TILE, ROW_TILE), ROW_TILE)
            squares = jnp.zeros((ROW_TILE, HEAD_DIM), jnp.float32)
            for head in range(heads):
                part = source[rows, head * HEAD_DIM : (head + 1) * HEAD_DIM].astype(jnp.float32)
                squares = squares + part * part
            power = jnp.sum(squares, axis=-1, keepdims=True) / width
            scale = lax.rsqrt(power + EPSILON)
            for head in range(heads):
                columns = slice(head * HEAD_DIM, (head + 1) * HEAD_DIM)
                part = source[rows, columns].astype(jnp.float32)
                target[head, rows, :] = (part * scale * gain[:, columns]).astype(jnp.bfloat16)
            return carry

        lax.fori_loop(0, BLOCK // ROW_TILE, rows_step, 0)

    spread(0, 0)
    loads[0].wait()
    loads[1].wait()
    normalise(q_in, q_gain, q_send)
    spread(1, 0)
    loads[2].wait()
    loads[3].wait()
    normalise(k_in, k_gain, k_send)
    spread(2, 0)
    for h in range(1, heads_dev):
        for kind in range(3):
            spread(kind, h)
    loads[4].wait()
    loads[5].wait()

    def landed(buffer, semaphore):
        others = buffer.at[pl.ds(0, n - 1)]
        pltpu.make_async_copy(others, others, semaphore).wait()

    def attend(h, block):
        filled = count_smem[block, me * heads_dev + h]
        queries = q_all[h][block]
        scores = []
        for slot in range(slot_count):
            tile = list_smem[slot, block, me * heads_dev + h]
            tile_scores = (
                lax.dot_general(
                    queries,
                    k_all[h][tile],
                    (((1,), (1,)), ((), ())),
                    preferred_element_type=jnp.float32,
                )
                * logit_scale
            )
            if slot > 0:
                tile_scores = jnp.where(
                    jnp.full(tile_scores.shape, filled, jnp.int32) > slot, tile_scores, -jnp.inf
                )
            scores.append(tile_scores)
        row_max = jnp.max(functools.reduce(jnp.maximum, scores), axis=-1, keepdims=True)
        weights = [jnp.exp(tile_scores - row_max) for tile_scores in scores]
        row_total = jnp.sum(functools.reduce(jnp.add, weights), axis=-1, keepdims=True)
        total = None
        for slot in range(slot_count):
            tile = list_smem[slot, block, me * heads_dev + h]
            product = jnp.dot(
                weights[slot].astype(jnp.bfloat16),
                v_all[h][tile],
                preferred_element_type=jnp.float32,
            )
            total = product if total is None else total + product
        return (total / row_total).astype(jnp.bfloat16)

    def returned(h, block):
        return pltpu.make_async_remote_copy(
            src_ref=o_send.at[h, block],
            dst_ref=out_columns(me * heads_dev + h),
            send_sem=back_send_sem.at[h],
            recv_sem=back_recv_sem.at[h],
            device_id={"seq": block},
            device_id_type=MESH,
        )

    def kept(h):
        return pltpu.make_async_copy(
            o_send.at[h, me], out_columns(me * heads_dev + h), own_sem.at[3, h]
        )

    last = heads_dev - 1
    for h in range(heads_dev):
        for kind in range(3):
            own_copy(kind, h).wait()
            landed(sources[kind][1][h], recv_sem.at[kind, h])

        def item(i, carry):
            block = partner(i)
            o_send[h, block] = attend(h, block)
            if h == last:
                returned(h, block).start()
            return carry

        lax.fori_loop(0, n - 1, item, 0, unroll=UNROLL)
        o_send[h, me] = attend(h, me)
        kept(h).start()
        if h == last - 1:
            for kind in range(3):
                landed(sources[kind][1][last], send_sem.at[kind, last])

            def give_back(i, carry):
                for done in range(last):
                    returned(done, partner(i)).start()
                return carry

            lax.fori_loop(0, n - 1, give_back, 0)

    for h in range(heads_dev):
        kept(h).wait()
        landed(o_send.at[h], back_recv_sem.at[h])
        landed(o_send.at[h], back_send_sem.at[h])
        if h < last or last == 0:
            for kind in range(3):
                landed(sources[kind][1][h], send_sem.at[kind, h])


UNROLL = 3


def fused(query, key_in, value, q_gain, k_gain, tile_list, tile_count):
    n = lax.axis_size("seq")
    tok_rows, row_width = query.shape
    head_count = row_width // HEAD_DIM
    heads_dev = head_count // n
    slot_count = tile_list.shape[-1]
    blocks = tile_list.shape[1]
    any_space = pl.BlockSpec(memory_space=pl.ANY)
    landing = (pltpu.VMEM((n, BLOCK, HEAD_DIM), jnp.bfloat16),) * heads_dev
    return pl.pallas_call(
        functools.partial(attention_kernel, n, heads_dev, slot_count),
        out_shape=jax.ShapeDtypeStruct((tok_rows, row_width), jnp.bfloat16),
        in_specs=[any_space] * 7,
        out_specs=any_space,
        scratch_shapes=[
            pltpu.SMEM((slot_count, blocks, head_count), jnp.int32),
            pltpu.SMEM((blocks, head_count), jnp.int32),
            pltpu.VMEM((1, row_width), jnp.float32),
            pltpu.VMEM((1, row_width), jnp.float32),
            pltpu.VMEM((tok_rows, row_width), jnp.bfloat16),
            pltpu.VMEM((tok_rows, row_width), jnp.bfloat16),
            pltpu.VMEM((head_count, BLOCK, HEAD_DIM), jnp.bfloat16),
            pltpu.VMEM((head_count, BLOCK, HEAD_DIM), jnp.bfloat16),
            landing,
            landing,
            landing,
            pltpu.VMEM((heads_dev, n, BLOCK, HEAD_DIM), jnp.bfloat16),
            pltpu.SemaphoreType.DMA((6,)),
            pltpu.SemaphoreType.DMA((4, heads_dev)),
            pltpu.SemaphoreType.DMA((3, heads_dev)),
            pltpu.SemaphoreType.DMA((3, heads_dev)),
            pltpu.SemaphoreType.DMA((heads_dev,)),
            pltpu.SemaphoreType.DMA((heads_dev,)),
        ],
        compiler_params=pltpu.CompilerParams(
            collective_id=0, has_side_effects=True, vmem_limit_bytes=40 * 1024 * 1024
        ),
        cost_estimate=pl.CostEstimate(
            flops=4 * heads_dev * n * slot_count * BLOCK * BLOCK * HEAD_DIM,
            bytes_accessed=8 * tok_rows * row_width,
            transcendentals=heads_dev * n * slot_count * BLOCK * BLOCK,
        ),
    )(
        *(
            pltpu.with_memory_space_constraint(operand, pltpu.HBM)
            for operand in (
                tile_list.transpose(2, 1, 0),
                tile_count.T,
                q_gain.reshape(1, row_width),
                k_gain.reshape(1, row_width),
                query,
                key_in,
                value,
            )
        )
    )


def rms_scaled(row_data, gain_row):
    values = row_data.astype(jnp.float32)
    power = jnp.mean(values * values, axis=-1, keepdims=True)
    return (values * lax.rsqrt(power + EPSILON) * gain_row).astype(jnp.bfloat16)


def exchanged(query, key_in, value, q_gain, k_gain, tile_list, tile_count):
    devices = lax.axis_size("seq")
    tok_rows, row_width = query.shape
    head_dim = HEAD_DIM
    block_rows = BLOCK
    head_count = row_width // head_dim
    replicas = max(1, devices // head_count)
    heads_dev = max(1, head_count // devices)
    group_count = head_count // heads_dev
    slot_count = tile_list.shape[-1]
    blocks = tile_list.shape[1]
    position = lax.axis_index("seq")
    residue = position % replicas
    head_group = position // replicas
    logit_scale = head_dim ** (-0.5)
    q_normed = rms_scaled(query, q_gain)
    k_normed = rms_scaled(key_in, k_gain)

    def whole_rows(row_data):
        split = row_data.reshape(tok_rows, group_count, 1, heads_dev, head_dim)
        spread = jnp.broadcast_to(split, (tok_rows, group_count, replicas, heads_dev, head_dim))
        return spread.transpose(1, 2, 3, 0, 4).reshape(devices, heads_dev, tok_rows, head_dim)

    stacked = jnp.stack([whole_rows(q_normed), whole_rows(k_normed), whole_rows(value)], axis=1)
    received = lax.all_to_all(stacked, "seq", split_axis=0, concat_axis=0, tiled=True)
    full_rows = received.transpose(1, 2, 0, 3, 4).reshape(
        3, heads_dev, devices * tok_rows, head_dim
    )
    own_blocks = blocks // replicas
    query_sets = full_rows[0].reshape(heads_dev, own_blocks, replicas, block_rows, head_dim)
    queries = lax.dynamic_index_in_dim(query_sets, residue, axis=2, keepdims=False)
    queries = queries.reshape(heads_dev * own_blocks, block_rows, head_dim)
    query_block = jnp.arange(own_blocks) * replicas + residue
    head_ids = head_group * heads_dev + jnp.arange(heads_dev)
    item_slots = (
        tile_list[head_ids][:, query_block] + (jnp.arange(heads_dev) * blocks)[:, None, None]
    )
    item_slots = item_slots.reshape(-1, slot_count)
    counts = tile_count[head_ids][:, query_block].reshape(-1)
    key_tiles_all = full_rows[1].reshape(heads_dev * blocks, block_rows, head_dim)
    value_tiles_all = full_rows[2].reshape(heads_dev * blocks, block_rows, head_dim)
    item_count = queries.shape[0]
    per_step = math.gcd(item_count, max(1, 512 // block_rows))

    def padded(q_items, tile_slots, filled):
        gathered_key_tiles = jnp.take(key_tiles_all, tile_slots, axis=0).reshape(
            per_step, slot_count * block_rows, head_dim
        )
        gathered_value_tiles = jnp.take(value_tiles_all, tile_slots, axis=0).reshape(
            per_step, slot_count * block_rows, head_dim
        )
        tile_scores = (
            jnp.einsum(
                "gqd,gkd->gqk", q_items, gathered_key_tiles, preferred_element_type=jnp.float32
            )
            * logit_scale
        )
        is_valid = jnp.repeat(
            jnp.arange(slot_count)[None, :] < filled[:, None], block_rows, axis=1
        )[:, None, :]
        row_max = jnp.max(jnp.where(is_valid, tile_scores, -jnp.inf), axis=-1, keepdims=True)
        weights_f = jnp.where(is_valid, jnp.exp(tile_scores - row_max), 0.0)
        row_total = jnp.sum(weights_f, axis=-1, keepdims=True)
        weighted_values = jnp.einsum(
            "gqk,gkd->gqd",
            weights_f.astype(jnp.bfloat16),
            gathered_value_tiles,
            preferred_element_type=jnp.float32,
        )
        return (weighted_values / row_total).astype(jnp.bfloat16)

    def attend(batch_in):
        q_items, tile_slots, filled = batch_in
        return padded(q_items, tile_slots, filled)

    steps_n = item_count // per_step
    outputs = lax.map(
        attend,
        (
            queries.reshape(steps_n, per_step, block_rows, head_dim),
            item_slots.reshape(steps_n, per_step, slot_count),
            counts.reshape(steps_n, per_step),
        ),
    )
    outputs = outputs.reshape(heads_dev, own_blocks, 1, block_rows, head_dim)
    chosen = (jnp.arange(replicas) == residue).astype(jnp.bfloat16)[None, None, :, None, None]
    placed = (
        (outputs * chosen).reshape(heads_dev, devices, tok_rows, head_dim).transpose(1, 0, 2, 3)
    )
    returned = lax.all_to_all(placed, "seq", split_axis=0, concat_axis=0, tiled=True)
    returned = returned.reshape(group_count, replicas, heads_dev, tok_rows, head_dim)
    combined = jnp.sum(returned.astype(jnp.float32), axis=1).astype(jnp.bfloat16)
    return combined.transpose(2, 0, 1, 3).reshape(tok_rows, row_width)


def per_device(query, key_in, value, q_gain, k_gain, tile_list, tile_count):
    devices = lax.axis_size("seq")
    tok_rows, row_width = query.shape
    head_count = row_width // HEAD_DIM
    one_block = tok_rows == BLOCK and tile_list.shape[1] == devices
    if devices > 1 and head_count % devices == 0 and one_block:
        return fused(query, key_in, value, q_gain, k_gain, tile_list, tile_count)
    return exchanged(query, key_in, value, q_gain, k_gain, tile_list, tile_count)


def solution(mesh):
    return jax.shard_map(
        per_device,
        mesh=mesh,
        in_specs=(
            P(("groups", "seq"), None),
            P(("groups", "seq"), None),
            P(("groups", "seq"), None),
            P(),
            P(),
            P(),
            P(),
        ),
        out_specs=P(("groups", "seq"), None),
        check_vma=False,
    )
```

```python
import functools
import math

import jax
import jax.numpy as jnp
from jax import lax
from jax.experimental import pallas as pl
from jax.experimental.pallas import tpu as pltpu
from jax.sharding import PartitionSpec as P

HEAD_DIM = 128
BLOCK = 128
ROW_TILE = 16
EPSILON = 1e-06
MESH = pl.DeviceIdType.MESH


def attention_kernel(
    n,
    heads_dev,
    slot_count,
    list_hbm,
    count_hbm,
    q_gain_hbm,
    k_gain_hbm,
    q_hbm,
    k_hbm,
    v_hbm,
    out,
    list_smem,
    count_smem,
    q_gain,
    k_gain,
    q_in,
    k_in,
    q_send,
    k_send,
    q_all,
    k_all,
    v_all,
    o_send,
    load_sem,
    own_sem,
    send_sem,
    recv_sem,
    back_send_sem,
    back_recv_sem,
):
    me = lax.axis_index("seq")
    heads = n * heads_dev
    width = heads * HEAD_DIM
    logit_scale = HEAD_DIM ** (-0.5)

    loads = [
        pltpu.make_async_copy(q_hbm, q_in, load_sem.at[0]),
        pltpu.make_async_copy(q_gain_hbm, q_gain, load_sem.at[1]),
        pltpu.make_async_copy(k_hbm, k_in, load_sem.at[2]),
        pltpu.make_async_copy(k_gain_hbm, k_gain, load_sem.at[3]),
        pltpu.make_async_copy(list_hbm, list_smem, load_sem.at[4]),
        pltpu.make_async_copy(count_hbm, count_smem, load_sem.at[5]),
    ]
    for load in loads:
        load.start()

    barrier = pltpu.get_barrier_semaphore()

    def greet(i, carry):
        peer = lax.rem(me + 1 + i, n)
        pl.semaphore_signal(barrier, inc=1, device_id={"seq": peer}, device_id_type=MESH)
        return carry

    lax.fori_loop(0, n - 1, greet, 0)
    pl.semaphore_wait(barrier, n - 1)

    def partner(i):
        return lax.rem(me + 1 + lax.rem(n // 2 - 1 + i, n - 1), n)

    def v_columns(head):
        return v_hbm.at[:, pl.ds(pl.multiple_of(head * HEAD_DIM, HEAD_DIM), heads_dev * HEAD_DIM)]

    def out_columns(head):
        return out.at[:, pl.ds(pl.multiple_of(head * HEAD_DIM, HEAD_DIM), HEAD_DIM)]

    sources = (
        (v_columns, (v_all,)),
        (lambda head: q_send.at[head], q_all),
        (lambda head: k_send.at[head], k_all),
    )

    def kinds(h):
        return range(3) if h == 0 else (1, 2)

    def own_copy(kind, h):
        source, landing = sources[kind]
        return pltpu.make_async_copy(
            source(me * heads_dev + h), landing[h].at[me], own_sem.at[kind, h]
        )

    def spread(kind, h):
        source, landing = sources[kind]

        def body(i, carry):
            peer = partner(i)
            pltpu.make_async_remote_copy(
                src_ref=source(peer * heads_dev + h),
                dst_ref=landing[h].at[me],
                send_sem=send_sem.at[kind, h],
                recv_sem=recv_sem.at[kind, h],
                device_id={"seq": peer},
                device_id_type=MESH,
            ).start()
            return carry

        lax.fori_loop(0, n - 1, body, 0)
        own_copy(kind, h).start()

    def normalise(source, gain, target):
        def rows_step(i, carry):
            rows = pl.ds(pl.multiple_of(i * ROW_TILE, ROW_TILE), ROW_TILE)
            squares = jnp.zeros((ROW_TILE, HEAD_DIM), jnp.float32)
            for head in range(heads):
                part = source[rows, head * HEAD_DIM : (head + 1) * HEAD_DIM].astype(jnp.float32)
                squares = squares + part * part
            power = jnp.sum(squares, axis=-1, keepdims=True) / width
            scale = lax.rsqrt(power + EPSILON)
            for head in range(heads):
                columns = slice(head * HEAD_DIM, (head + 1) * HEAD_DIM)
                part = source[rows, columns].astype(jnp.float32)
                target[head, rows, :] = (part * scale * gain[:, columns]).astype(jnp.bfloat16)
            return carry

        lax.fori_loop(0, BLOCK // ROW_TILE, rows_step, 0)

    spread(0, 0)
    loads[0].wait()
    loads[1].wait()
    normalise(q_in, q_gain, q_send)
    spread(1, 0)
    loads[2].wait()
    loads[3].wait()
    normalise(k_in, k_gain, k_send)
    spread(2, 0)
    for h in range(1, heads_dev):
        for kind in kinds(h):
            spread(kind, h)
    loads[4].wait()
    loads[5].wait()

    def landed(buffer, semaphore):
        others = buffer.at[pl.ds(0, n - 1)]
        pltpu.make_async_copy(others, others, semaphore).wait()

    def attend(h, block):
        filled = count_smem[block, me * heads_dev + h]
        queries = q_all[h][block]
        scores = []
        for slot in range(slot_count):
            tile = list_smem[slot, block, me * heads_dev + h]
            tile_scores = (
                lax.dot_general(
                    queries,
                    k_all[h][tile],
                    (((1,), (1,)), ((), ())),
                    preferred_element_type=jnp.float32,
                )
                * logit_scale
            )
            if slot > 0:
                tile_scores = jnp.where(
                    jnp.full(tile_scores.shape, filled, jnp.int32) > slot, tile_scores, -jnp.inf
                )
            scores.append(tile_scores)
        row_max = jnp.max(functools.reduce(jnp.maximum, scores), axis=-1, keepdims=True)
        weights = [jnp.exp(tile_scores - row_max) for tile_scores in scores]
        row_total = jnp.sum(functools.reduce(jnp.add, weights), axis=-1, keepdims=True)
        total = None
        for slot in range(slot_count):
            tile = list_smem[slot, block, me * heads_dev + h]
            product = jnp.dot(
                weights[slot].astype(jnp.bfloat16),
                v_all[tile, :, h * HEAD_DIM : (h + 1) * HEAD_DIM],
                preferred_element_type=jnp.float32,
            )
            total = product if total is None else total + product
        return (total / row_total).astype(jnp.bfloat16)

    def returned(h, block):
        return pltpu.make_async_remote_copy(
            src_ref=o_send.at[h, block],
            dst_ref=out_columns(me * heads_dev + h),
            send_sem=back_send_sem.at[h],
            recv_sem=back_recv_sem.at[h],
            device_id={"seq": block},
            device_id_type=MESH,
        )

    def kept(h):
        return pltpu.make_async_copy(
            o_send.at[h, me], out_columns(me * heads_dev + h), own_sem.at[3, h]
        )

    last = heads_dev - 1
    for h in range(heads_dev):
        for kind in kinds(h):
            own_copy(kind, h).wait()
            landed(sources[kind][1][h], recv_sem.at[kind, h])

        def item(i, carry):
            block = partner(i)
            o_send[h, block] = attend(h, block)
            if h == last:
                returned(h, block).start()
            return carry

        lax.fori_loop(0, n - 1, item, 0, unroll=UNROLL)
        o_send[h, me] = attend(h, me)
        kept(h).start()
        if h == last - 1:
            for kind in kinds(last):
                landed(sources[kind][1][last], send_sem.at[kind, last])

            def give_back(i, carry):
                for done in range(last):
                    returned(done, partner(i)).start()
                return carry

            lax.fori_loop(0, n - 1, give_back, 0)

    for h in range(heads_dev):
        kept(h).wait()
        landed(o_send.at[h], back_recv_sem.at[h])
        landed(o_send.at[h], back_send_sem.at[h])
        if h < last or last == 0:
            for kind in kinds(h):
                landed(sources[kind][1][h], send_sem.at[kind, h])


UNROLL = 3


def fused(query, key_in, value, q_gain, k_gain, tile_list, tile_count):
    n = lax.axis_size("seq")
    tok_rows, row_width = query.shape
    head_count = row_width // HEAD_DIM
    heads_dev = head_count // n
    slot_count = tile_list.shape[-1]
    blocks = tile_list.shape[1]
    any_space = pl.BlockSpec(memory_space=pl.ANY)
    landing = (pltpu.VMEM((n, BLOCK, HEAD_DIM), jnp.bfloat16),) * heads_dev
    return pl.pallas_call(
        functools.partial(attention_kernel, n, heads_dev, slot_count),
        out_shape=jax.ShapeDtypeStruct((tok_rows, row_width), jnp.bfloat16),
        in_specs=[any_space] * 7,
        out_specs=any_space,
        scratch_shapes=[
            pltpu.SMEM((slot_count, blocks, head_count), jnp.int32),
            pltpu.SMEM((blocks, head_count), jnp.int32),
            pltpu.VMEM((1, row_width), jnp.float32),
            pltpu.VMEM((1, row_width), jnp.float32),
            pltpu.VMEM((tok_rows, row_width), jnp.bfloat16),
            pltpu.VMEM((tok_rows, row_width), jnp.bfloat16),
            pltpu.VMEM((head_count, BLOCK, HEAD_DIM), jnp.bfloat16),
            pltpu.VMEM((head_count, BLOCK, HEAD_DIM), jnp.bfloat16),
            landing,
            landing,
            pltpu.VMEM((n, BLOCK, heads_dev * HEAD_DIM), jnp.bfloat16),
            pltpu.VMEM((heads_dev, n, BLOCK, HEAD_DIM), jnp.bfloat16),
            pltpu.SemaphoreType.DMA((6,)),
            pltpu.SemaphoreType.DMA((4, heads_dev)),
            pltpu.SemaphoreType.DMA((3, heads_dev)),
            pltpu.SemaphoreType.DMA((3, heads_dev)),
            pltpu.SemaphoreType.DMA((heads_dev,)),
            pltpu.SemaphoreType.DMA((heads_dev,)),
        ],
        compiler_params=pltpu.CompilerParams(
            collective_id=0, has_side_effects=True, vmem_limit_bytes=40 * 1024 * 1024
        ),
        cost_estimate=pl.CostEstimate(
            flops=4 * heads_dev * n * slot_count * BLOCK * BLOCK * HEAD_DIM,
            bytes_accessed=8 * tok_rows * row_width,
            transcendentals=heads_dev * n * slot_count * BLOCK * BLOCK,
        ),
    )(
        *(
            pltpu.with_memory_space_constraint(operand, pltpu.HBM)
            for operand in (
                tile_list.transpose(2, 1, 0),
                tile_count.T,
                q_gain.reshape(1, row_width),
                k_gain.reshape(1, row_width),
                query,
                key_in,
                value,
            )
        )
    )


def rms_scaled(row_data, gain_row):
    values = row_data.astype(jnp.float32)
    power = jnp.mean(values * values, axis=-1, keepdims=True)
    return (values * lax.rsqrt(power + EPSILON) * gain_row).astype(jnp.bfloat16)


def exchanged(query, key_in, value, q_gain, k_gain, tile_list, tile_count):
    devices = lax.axis_size("seq")
    tok_rows, row_width = query.shape
    head_dim = HEAD_DIM
    block_rows = BLOCK
    head_count = row_width // head_dim
    replicas = max(1, devices // head_count)
    heads_dev = max(1, head_count // devices)
    group_count = head_count // heads_dev
    slot_count = tile_list.shape[-1]
    blocks = tile_list.shape[1]
    position = lax.axis_index("seq")
    residue = position % replicas
    head_group = position // replicas
    logit_scale = head_dim ** (-0.5)
    q_normed = rms_scaled(query, q_gain)
    k_normed = rms_scaled(key_in, k_gain)

    def whole_rows(row_data):
        split = row_data.reshape(tok_rows, group_count, 1, heads_dev, head_dim)
        spread = jnp.broadcast_to(split, (tok_rows, group_count, replicas, heads_dev, head_dim))
        return spread.transpose(1, 2, 3, 0, 4).reshape(devices, heads_dev, tok_rows, head_dim)

    stacked = jnp.stack([whole_rows(q_normed), whole_rows(k_normed), whole_rows(value)], axis=1)
    received = lax.all_to_all(stacked, "seq", split_axis=0, concat_axis=0, tiled=True)
    full_rows = received.transpose(1, 2, 0, 3, 4).reshape(
        3, heads_dev, devices * tok_rows, head_dim
    )
    own_blocks = blocks // replicas
    query_sets = full_rows[0].reshape(heads_dev, own_blocks, replicas, block_rows, head_dim)
    queries = lax.dynamic_index_in_dim(query_sets, residue, axis=2, keepdims=False)
    queries = queries.reshape(heads_dev * own_blocks, block_rows, head_dim)
    query_block = jnp.arange(own_blocks) * replicas + residue
    head_ids = head_group * heads_dev + jnp.arange(heads_dev)
    item_slots = (
        tile_list[head_ids][:, query_block] + (jnp.arange(heads_dev) * blocks)[:, None, None]
    )
    item_slots = item_slots.reshape(-1, slot_count)
    counts = tile_count[head_ids][:, query_block].reshape(-1)
    key_tiles_all = full_rows[1].reshape(heads_dev * blocks, block_rows, head_dim)
    value_tiles_all = full_rows[2].reshape(heads_dev * blocks, block_rows, head_dim)
    item_count = queries.shape[0]
    per_step = math.gcd(item_count, max(1, 512 // block_rows))

    def padded(q_items, tile_slots, filled):
        gathered_key_tiles = jnp.take(key_tiles_all, tile_slots, axis=0).reshape(
            per_step, slot_count * block_rows, head_dim
        )
        gathered_value_tiles = jnp.take(value_tiles_all, tile_slots, axis=0).reshape(
            per_step, slot_count * block_rows, head_dim
        )
        tile_scores = (
            jnp.einsum(
                "gqd,gkd->gqk", q_items, gathered_key_tiles, preferred_element_type=jnp.float32
            )
            * logit_scale
        )
        is_valid = jnp.repeat(
            jnp.arange(slot_count)[None, :] < filled[:, None], block_rows, axis=1
        )[:, None, :]
        row_max = jnp.max(jnp.where(is_valid, tile_scores, -jnp.inf), axis=-1, keepdims=True)
        weights_f = jnp.where(is_valid, jnp.exp(tile_scores - row_max), 0.0)
        row_total = jnp.sum(weights_f, axis=-1, keepdims=True)
        weighted_values = jnp.einsum(
            "gqk,gkd->gqd",
            weights_f.astype(jnp.bfloat16),
            gathered_value_tiles,
            preferred_element_type=jnp.float32,
        )
        return (weighted_values / row_total).astype(jnp.bfloat16)

    def attend(batch_in):
        q_items, tile_slots, filled = batch_in
        return padded(q_items, tile_slots, filled)

    steps_n = item_count // per_step
    outputs = lax.map(
        attend,
        (
            queries.reshape(steps_n, per_step, block_rows, head_dim),
            item_slots.reshape(steps_n, per_step, slot_count),
            counts.reshape(steps_n, per_step),
        ),
    )
    outputs = outputs.reshape(heads_dev, own_blocks, 1, block_rows, head_dim)
    chosen = (jnp.arange(replicas) == residue).astype(jnp.bfloat16)[None, None, :, None, None]
    placed = (
        (outputs * chosen).reshape(heads_dev, devices, tok_rows, head_dim).transpose(1, 0, 2, 3)
    )
    returned = lax.all_to_all(placed, "seq", split_axis=0, concat_axis=0, tiled=True)
    returned = returned.reshape(group_count, replicas, heads_dev, tok_rows, head_dim)
    combined = jnp.sum(returned.astype(jnp.float32), axis=1).astype(jnp.bfloat16)
    return combined.transpose(2, 0, 1, 3).reshape(tok_rows, row_width)


def per_device(query, key_in, value, q_gain, k_gain, tile_list, tile_count):
    devices = lax.axis_size("seq")
    tok_rows, row_width = query.shape
    head_count = row_width // HEAD_DIM
    one_block = tok_rows == BLOCK and tile_list.shape[1] == devices
    if devices > 1 and head_count % devices == 0 and one_block:
        return fused(query, key_in, value, q_gain, k_gain, tile_list, tile_count)
    return exchanged(query, key_in, value, q_gain, k_gain, tile_list, tile_count)


def solution(mesh):
    return jax.shard_map(
        per_device,
        mesh=mesh,
        in_specs=(
            P(("groups", "seq"), None),
            P(("groups", "seq"), None),
            P(("groups", "seq"), None),
            P(),
            P(),
            P(),
            P(),
        ),
        out_specs=P(("groups", "seq"), None),
        check_vma=False,
    )
```
